128 devices in a mesh: mem: 64 (over z, y, x), grp: 2 (over core).
Axes of the slice: x: 4, y: 4, z: 4, core: 2. Of those that a mesh axis runs over, the one named last changes fastest.
Arguments:
- queries: bfloat16 [18432, 1024], P(('mem', 'grp')), may hold values from -2 to 2
- keys: bfloat16 [18432, 1024], P(('mem', 'grp')), may hold values from -10 to 10
- labels: int32 [18432], P(('mem', 'grp')), may hold values from 0 to 63
- memory: bfloat16 [262144, 1024], P(('mem', 'grp')), may hold values from -40 to 40
- mem_labels: int32 [262144], P(('mem', 'grp')), may hold values from 0 to 63
- pairs: int32 [2304, 3], P(('mem', 'grp')), may hold values from 0 to 127, all different within a row; in each aligned block of 18 rows (0 to 17, 18 to 35, ...) at most 2 rows name the same one
- offset: int32 [1], replicated, may hold values from 0 to 2047
Outputs:
- loss: float32 [18432], P(('mem', 'grp'))
- grad: float32 [18432, 1024], P(('mem', 'grp'))
- new_memory: bfloat16 [262144, 1024], P(('mem', 'grp'))
The draws below stay inside these ranges and needn't reach their ends.
Inputs may be any that keep to these rules, and one draw needn't show every extreme that they name: `pairs`: each row names 3 different shards; among the 18 rows of one device no shard is named more than 2 times, and in some devices one shard exactly 2 times.
All inputs are finite; a program needn't handle non-finite values.
Results may differ from the reference program's by a relative error of at most 0.0024.
Values may be sent and summed in bfloat16 or wider, within the bound.
No kernel may reach another device: no remote copies, remote signals or barrier semaphores. Data moves between devices by JAX's collectives and lax.ppermute only.
A program may use at most 128 MiB of HBM per device.

```python
import math
import jax
import jax.numpy as jnp
import numpy as np
from jax import lax

E = 1024
SLOT_DEV = 2048
BLK = 8
NB = 18
K = 3
CAP = 2
CLUSTERS = 64
SHARDS = 128
BAT_DEV = 144
BATCH = 18432
BLOCKS = 2304
MEMORY = 262144


QUERY_SCALE = 0.047


KEY_GAIN = 2.0


def sample_rows(key, strong):
    base = jax.random.truncated_normal(jax.random.fold_in(key, 101), -6.0, 6.0, (BATCH, E), jnp.float32)
    noise = jax.random.truncated_normal(jax.random.fold_in(key, 102), -6.0, 6.0, (BATCH, E), jnp.float32)
    row_index = jnp.arange(BATCH, dtype=jnp.int32)[:, None]
    marked = (row_index % 61 == 0).astype(jnp.float32) * strong
    query = base * QUERY_SCALE
    query = query * (1.0 - marked)
    return (query, noise)


def draw_queries(key, part):
    query, noise = sample_rows(key, 0.0)
    return query.astype(jnp.bfloat16)


def draw_keys(key, part):
    query, noise = sample_rows(key, 0.0)
    return (KEY_GAIN * query + noise).astype(jnp.bfloat16)


def draw_memory(key, part):
    key = jax.random.fold_in(key, 7)
    first, second, third = jax.random.split(key, 3)
    row_scale = jnp.exp(jax.random.uniform(first, (MEMORY, 1), jnp.float32, -1.15, 1.15))
    col_scale = jnp.exp(jax.random.uniform(second, (1, E), jnp.float32, -0.7, 0.7))
    values = jax.random.truncated_normal(third, -6.0, 6.0, (MEMORY, E), jnp.float32) * col_scale
    return (row_scale * values).astype(jnp.bfloat16)


def set_ends(entries, stream_key, low, high):
    longest = entries.shape.index(max(entries.shape))
    spots = []
    for shift in (0, 1):
        where = [jax.random.randint(jax.random.fold_in(stream_key, axis), (), 0, length) for axis, length in enumerate(entries.shape)]
        where[longest] = (where[longest] + shift) % entries.shape[longest]
        spots.append(tuple(where))
    return entries.at[spots[0]].set(low).at[spots[1]].set(high)


def shared_out(rng, own, number, rows, count, top, bound, lean):
    order = jax.random.permutation(rng, count)
    crowded, usual = portions_of(count, rows * top, bound, lean, True), portions_of(count, rows * top, bound, lean, False)
    places = jnp.arange(count)

    def named(sizes, turn):
        used = int((sizes > 0).sum())
        fixed = max(1, used // 4)
        moved = fixed + (places - fixed + turn * (used - fixed)) % max(1, count - fixed)
        return jnp.zeros((count,), jnp.int32).at[order[jnp.where(places < fixed, places, moved)]].set(jnp.asarray(sizes, jnp.int32))

    sizes = jnp.where(number % 4 == 0, named(crowded, number // 4), named(usual, number - number // 4 - 1))
    mixed = jax.random.permutation(jax.random.fold_in(own, 3), count)
    source_of, sink = mixed[0:count // 2 * 2:2], mixed[1:count // 2 * 2:2]
    room = jnp.minimum(sizes[source_of] - 1, bound - sizes[sink]) // 2
    room = jnp.where((source_of == order[0]) | (sink == order[0]) | (sizes[sink] == 0), 0, jnp.maximum(room, 0))
    moved = jax.random.randint(jax.random.fold_in(own, 4), (count // 2,), 0, 1 << 20) % (room + 1)
    sizes = sizes.at[source_of].add(-moved).at[sink].add(moved)
    members = jnp.searchsorted(jnp.cumsum(sizes), jnp.arange(rows * top), side="right").astype(jnp.int32)
    grid = members.reshape(top, rows).T
    grid = grid[jax.random.permutation(jax.random.fold_in(own, 1), rows)]
    turn = jax.random.randint(jax.random.fold_in(own, 2), (rows, 1), 0, top)
    return jnp.take_along_axis(grid, (jnp.arange(top)[None, :] + turn) % top, axis=1)


def portions_of(number_of, total, bound, lean, full):
    loads = [(1 << 20) // math.isqrt(grade ** lean) + 1 for grade in range(1, number_of + 1)]
    largest = bound if full else min(bound, max(-(-total // number_of), total * loads[0] // sum(loads)))
    least = 1 if total - largest >= number_of - 1 else 0
    given, surplus = [largest] + [least] * (number_of - 1), total - largest - least * (number_of - 1)
    while surplus > 0:
        movable = [i for i in range(1, number_of) if given[i] < largest] or [i for i in range(1, number_of) if given[i] < bound]
        whole, remaining = sum([loads[i] for i in movable]), surplus
        for i in movable:
            more = min(bound - given[i], max(1, remaining * loads[i] // whole), surplus)
            given[i] = given[i] + more
            surplus = surplus - more
    return np.array(given)


def setup_inputs(seed: int = 0) -> dict:
    key_of = jax.random.split(jax.random.key(seed), 8)
    queries = draw_queries(jax.random.fold_in(key_of[7], 71), 0)
    keys = draw_keys(jax.random.fold_in(key_of[7], 71), 0)
    labels = set_ends(jax.random.randint(key_of[2], (BATCH,), 0, CLUSTERS), jax.random.fold_in(key_of[2], 1), 0, CLUSTERS - 1).astype(jnp.int32)
    memory = draw_memory(jax.random.fold_in(key_of[7], 71), 0)
    mem_labels = set_ends(jax.random.randint(key_of[4], (MEMORY,), 0, CLUSTERS), jax.random.fold_in(key_of[4], 1), 0, CLUSTERS - 1).astype(jnp.int32)
    pairs_keys = jax.random.split(jax.random.fold_in(key_of[5], 1), BLOCKS // NB)
    pairs_turns = jax.random.permutation(jax.random.fold_in(key_of[5], 3), BLOCKS // NB)
    pairs = jax.vmap(lambda own, number: shared_out(jax.random.fold_in(key_of[5], 2), own, number, NB, SHARDS, K, CAP, 2))(pairs_keys, pairs_turns).reshape((BLOCKS, K))
    offset = jax.random.randint(key_of[6], (1,), 0, SLOT_DEV).astype(jnp.int32)
    return {"queries": queries, "keys": keys, "labels": labels, "memory": memory, "mem_labels": mem_labels, "pairs": pairs, "offset": offset}


def shard_terms(rows_query, rows_label, shard_rows, shard_labels):
    scores = lax.dot_general(rows_query, shard_rows, (((1,), (1,)), ((), ())), preferred_element_type=jnp.float32)
    local_max = jnp.max(scores, axis=1)
    weights = jnp.exp(scores - local_max[:, None])
    positive = (rows_label[:, None] == shard_labels[None, :]).astype(jnp.float32)
    positive_weights = weights * positive
    part_all = jnp.sum(weights, axis=1)
    part_pos = jnp.sum(positive_weights, axis=1)
    stacked = jnp.concatenate([weights, positive_weights], axis=0).astype(jnp.bfloat16)
    sums = jnp.dot(stacked, shard_rows, preferred_element_type=jnp.float32)
    row_count = rows_query.shape[0]
    return local_max, part_all, part_pos, sums[:row_count], sums[row_count:]


def combine(query_part, key_part, maxima, part_all, part_pos, sum_all, sum_pos):
    own_score = jnp.einsum('...e,...e->...', query_part.astype(jnp.float32), key_part.astype(jnp.float32))
    top_score = jnp.maximum(own_score, jnp.max(maxima, axis=-2))
    scales = jnp.exp(maxima - top_score[..., None, :])
    own_weight = jnp.exp(own_score - top_score)
    total_all = own_weight + jnp.sum(scales * part_all, axis=-2)
    total_pos = own_weight + jnp.sum(scales * part_pos, axis=-2)
    loss_rows = jnp.log(total_all) - jnp.log(total_pos)
    weighted = scales[..., None] * (sum_all / total_all[..., None, :, None] - sum_pos / total_pos[..., None, :, None])
    own_factor = own_weight * (1.0 / total_all - 1.0 / total_pos)
    gradient = jnp.sum(weighted, axis=-3) + own_factor[..., None] * key_part.astype(jnp.float32)
    return loss_rows, gradient


def cycle_write(shard, shard_keys, start):
    slot_count = shard.shape[0]
    key_count = shard_keys.shape[0]
    distance = (jnp.arange(slot_count, dtype=jnp.int32) - start) % slot_count
    source = shard_keys[jnp.minimum(distance, key_count - 1)]
    return jnp.where((distance < key_count)[:, None], source, shard)


def reference(queries, keys, labels, memory, mem_labels, pairs, offset):
    shard_rows = memory.reshape(SHARDS, SLOT_DEV, E)
    shard_labels = mem_labels.reshape(SHARDS, SLOT_DEV)

    def one_block(operands):
        block_query, block_keys, block_labels, targets = operands
        pieces = [shard_terms(block_query, block_labels, shard_rows[targets[position]], shard_labels[targets[position]]) for position in range(K)]
        stacked = [jnp.stack([piece[member] for piece in pieces]) for member in range(5)]
        return combine(block_query, block_keys, stacked[0], stacked[1], stacked[2], stacked[3], stacked[4])

    loss_rows, gradient = lax.map(one_block, (queries.reshape(BLOCKS, BLK, E), keys.reshape(BLOCKS, BLK, E), labels.reshape(BLOCKS, BLK), pairs))
    start = offset[0].astype(jnp.int32)

    def write_shard(shard, shard_keys):
        return cycle_write(shard, shard_keys, start)

    written = jax.vmap(write_shard)(shard_rows, keys.reshape(SHARDS, BAT_DEV, E))
    return loss_rows.reshape(BATCH), gradient.reshape(BATCH, E), written.reshape(MEMORY, E)
```

```python
import jax
import jax.numpy as jnp
from jax import lax
from jax.experimental import pallas as pl
from jax.experimental.pallas import tpu as pltpu
from jax.sharding import PartitionSpec as P

CAP = 2
F32 = jnp.float32
BF16 = jnp.bfloat16
I32 = jnp.int32
AXES = ("mem", "grp")
LANES = 128
VMEM = 56 * 1024 * 1024
EXACT = lax.Precision.HIGHEST


def iota(shape, axis):
    return lax.broadcasted_iota(I32, shape, axis)


def targets(pairs_ref, k, block_of):
    out = jnp.zeros(block_of.shape, I32)
    for b in range(pairs_ref.shape[0]):
        out = jnp.where(block_of == b, pairs_ref[b, k], out)
    return out


def spread(packed, rows):
    n = packed.shape[0]
    return jnp.broadcast_to(packed[:, None, :], (n, 16, LANES)).reshape(rows, LANES)


def column_of(wide, group):
    rows = wide.shape[0]
    pick = iota((rows, LANES), 1) == group * 16 + (iota((rows, LANES), 0) & 15)
    return jnp.sum(jnp.where(pick, wide, 0.0), axis=1, keepdims=True)


def pack_kernel(pairs_ref, label_ref, query_ref, send_ref, send_label_ref):
    step = pl.program_id(0)
    rows_dev = query_ref.shape[0]
    fanout = pairs_ref.shape[1]
    lane = iota((1, rows_dev), 1)
    shard = iota((16, rows_dev), 0) + step * 16
    match = jnp.zeros((16, rows_dev), jnp.bool_)
    for k in range(fanout):
        match = match | (targets(pairs_ref, k, lane >> 3) == shard)
    match_f = match.astype(F32)
    before = (iota((rows_dev, rows_dev), 0) >> 3) < (iota((rows_dev, rows_dev), 1) >> 3)
    before = before & ((iota((rows_dev, rows_dev), 0) & 7) == 0)
    earlier = jnp.dot(match_f.astype(BF16), before.astype(F32).astype(BF16), preferred_element_type=F32)
    first = jnp.where(earlier < 0.5, match_f, 0.0)
    second = match_f - first
    place = iota((16, 16, rows_dev), 1)
    chosen = jnp.where(place < 8, first[:, None, :], second[:, None, :])
    chosen = jnp.where((place & 7) == (iota((16, 16, rows_dev), 2) & 7), chosen, 0.0)
    chosen_rows = chosen.reshape(256, rows_dev).astype(BF16)
    send_ref[...] = jnp.dot(chosen_rows, query_ref[...], preferred_element_type=F32).astype(BF16)
    row_label = jnp.sum(chosen * label_ref[...][None].astype(F32), axis=2)
    send_label_ref[...] = jnp.concatenate([row_label, jnp.zeros((16, LANES - 16), F32)], axis=1)


def pack(pairs, labels, queries, shards):
    rows_dev, width = queries.shape
    return pl.pallas_call(
        pack_kernel,
        grid=(shards // 16,),
        in_specs=[
            pl.BlockSpec(memory_space=pltpu.SMEM),
            pl.BlockSpec((1, rows_dev), lambda i: (0, 0)),
            pl.BlockSpec((rows_dev, width), lambda i: (0, 0)),
        ],
        out_specs=[
            pl.BlockSpec((256, width), lambda i: (i, 0)),
            pl.BlockSpec((16, LANES), lambda i: (i, 0)),
        ],
        out_shape=[
            jax.ShapeDtypeStruct((shards * 16, width), BF16),
            jax.ShapeDtypeStruct((shards, LANES), F32),
        ],
        compiler_params=pltpu.CompilerParams(vmem_limit_bytes=VMEM),
        name="pack",
    )(pairs, labels.reshape(1, rows_dev), queries)


def score_kernel(query_ref, label_ref, memory_ref, slot_label_ref, weight_ref, stat_ref):
    rows = query_ref.shape[0]
    scores = lax.dot_general(
        query_ref[...], memory_ref[...], (((1,), (1,)), ((), ())), preferred_element_type=F32
    )
    top = jnp.max(scores, axis=1, keepdims=True)
    weights = jnp.exp(scores - top)
    row_label = column_of(spread(label_ref[...], rows), 0)
    same = row_label == slot_label_ref[...].astype(F32)
    part_all = jnp.sum(weights, axis=1, keepdims=True)
    part_pos = jnp.sum(jnp.where(same, weights, 0.0), axis=1, keepdims=True)
    weight_ref[...] = weights.astype(BF16)
    lane = iota((rows, LANES), 1)
    place = iota((rows, LANES), 0) & 15
    wide = jnp.where(lane == place, top, 0.0)
    wide = jnp.where(lane == place + 16, part_all, wide)
    wide = jnp.where(lane == place + 32, part_pos, wide)
    stat_ref[...] = jnp.sum(wide.reshape(rows // 16, 16, LANES), axis=1)


def score(rows_query, rows_label, memory, slot_label):
    total, width = rows_query.shape
    slots = memory.shape[0]
    step = 256
    return pl.pallas_call(
        score_kernel,
        grid=(total // step,),
        in_specs=[
            pl.BlockSpec((step, width), lambda i: (i, 0)),
            pl.BlockSpec((step // 16, LANES), lambda i: (i, 0)),
            pl.BlockSpec((slots, width), lambda i: (0, 0)),
            pl.BlockSpec((1, slots), lambda i: (0, 0)),
        ],
        out_specs=[
            pl.BlockSpec((step, slots), lambda i: (i, 0)),
            pl.BlockSpec((step // 16, LANES), lambda i: (i, 0)),
        ],
        out_shape=[
            jax.ShapeDtypeStruct((total, slots), BF16),
            jax.ShapeDtypeStruct((total // 16, LANES), F32),
        ],
        compiler_params=pltpu.CompilerParams(vmem_limit_bytes=VMEM),
        cost_estimate=pl.CostEstimate(
            flops=2 * total * slots * width, bytes_accessed=16 << 20, transcendentals=total * slots
        ),
        name="score",
    )(rows_query, rows_label, memory, slot_label)


def sums_kernel(weight_ref, label_ref, memory_ref, slot_label_ref, all_ref, pos_ref):
    rows = weight_ref.shape[0]
    weights = weight_ref[...]
    row_label = column_of(spread(label_ref[...], rows), 0)
    same = row_label == slot_label_ref[...].astype(F32)
    positive = jnp.where(same, weights.astype(F32), 0.0).astype(BF16)
    rows_memory = memory_ref[...]
    all_ref[...] = jnp.dot(weights, rows_memory, preferred_element_type=F32)
    pos_ref[...] = jnp.dot(positive, rows_memory, preferred_element_type=F32)


def sums(weights, rows_label, memory, slot_label, first, count):
    slots, width = memory.shape
    step = 256
    lead = first // step
    return pl.pallas_call(
        sums_kernel,
        grid=(count // step,),
        in_specs=[
            pl.BlockSpec((step, slots), lambda i: (i + lead, 0)),
            pl.BlockSpec((step // 16, LANES), lambda i: (i + lead, 0)),
            pl.BlockSpec((slots, width), lambda i: (0, 0)),
            pl.BlockSpec((1, slots), lambda i: (0, 0)),
        ],
        out_specs=[
            pl.BlockSpec((step, width), lambda i: (i, 0)),
            pl.BlockSpec((step, width), lambda i: (i, 0)),
        ],
        out_shape=[jax.ShapeDtypeStruct((count, width), F32)] * 2,
        compiler_params=pltpu.CompilerParams(vmem_limit_bytes=VMEM),
        cost_estimate=pl.CostEstimate(
            flops=4 * count * slots * width, bytes_accessed=16 << 20, transcendentals=0
        ),
        name="sums",
    )(weights, rows_label, memory, slot_label)


def total_kernel(pairs_ref, query_ref, key_ref, stat_ref, loss_ref, factor_ref, back_ref):
    rows = query_ref.shape[0]
    fanout = pairs_ref.shape[1]
    own = jnp.sum(query_ref[...].astype(F32) * key_ref[...].astype(F32), axis=1, keepdims=True)
    stat = stat_ref[...]
    stat_slot = (iota(stat.shape, 1) >> 3) & 1

    down_block = iota((rows, 1), 0) >> 3
    down_match = [
        (targets(pairs_ref, k, down_block) == iota((rows, LANES), 1)).astype(F32) for k in range(fanout)
    ]
    side = (rows, rows)
    earlier_down = ((iota(side, 1) >> 3) < (iota(side, 0) >> 3)) & ((iota(side, 1) & 7) == 0)
    down_count = jnp.dot(
        earlier_down.astype(F32).astype(BF16),
        sum(down_match[1:], down_match[0]).astype(BF16),
        preferred_element_type=F32,
    )
    lane = iota((rows, LANES), 1)
    mine = (lane & 7) == (iota((rows, LANES), 0) & 7)
    maxima, alls, poss = [], [], []
    for k in range(fanout):
        wide = jnp.zeros((rows, LANES), F32)
        for s in range(CAP):
            mask = jnp.where(down_count == s, down_match[k], 0.0)
            wide = wide + jnp.dot(
                mask, jnp.where(stat_slot == s, stat, 0.0), precision=EXACT, preferred_element_type=F32
            )
        for group, into in enumerate((maxima, alls, poss)):
            pick = mine & ((lane >> 4) == group)
            into.append(jnp.sum(jnp.where(pick, wide, 0.0), axis=1, keepdims=True))
    top = own
    for value in maxima:
        top = jnp.maximum(top, value)
    own_weight = jnp.exp(own - top)
    scales = [jnp.exp(value - top) for value in maxima]
    total_all, total_pos = own_weight, own_weight
    for k in range(fanout):
        total_all = total_all + scales[k] * alls[k]
        total_pos = total_pos + scales[k] * poss[k]
    loss = jnp.log(total_all) - jnp.log(total_pos)
    loss_ref[...] = jnp.sum(jnp.where(iota(side, 0) == iota(side, 1), loss, 0.0), axis=0, keepdims=True)
    factor_ref[...] = own_weight * (1.0 / total_all - 1.0 / total_pos)

    across_block = iota((1, rows), 1) >> 3
    across_match = [
        (targets(pairs_ref, k, across_block) == iota((LANES, rows), 0)).astype(F32) for k in range(fanout)
    ]
    earlier_across = ((iota(side, 0) >> 3) < (iota(side, 1) >> 3)) & ((iota(side, 0) & 7) == 0)
    across_count = jnp.dot(
        sum(across_match[1:], across_match[0]).astype(BF16),
        earlier_across.astype(F32).astype(BF16),
        preferred_element_type=F32,
    )
    back = jnp.zeros((LANES, LANES), F32)
    for k in range(fanout):
        factor_all, factor_pos = scales[k] / total_all, scales[k] / total_pos
        for s in range(CAP):
            mask = jnp.where(across_count == s, across_match[k], 0.0)
            value = jnp.where((lane >> 3) == s, factor_all, 0.0)
            value = jnp.where((lane >> 3) == 2 + s, factor_pos, value)
            value = jnp.where(mine, value, 0.0)
            back = back + jnp.dot(mask, value, precision=EXACT, preferred_element_type=F32)
    back_ref[...] = back


def totals(pairs, queries, keys, stat):
    rows = queries.shape[0]
    return pl.pallas_call(
        total_kernel,
        in_specs=[pl.BlockSpec(memory_space=pltpu.SMEM)] + [pl.BlockSpec(memory_space=pltpu.VMEM)] * 3,
        out_specs=[pl.BlockSpec(memory_space=pltpu.VMEM)] * 3,
        out_shape=[
            jax.ShapeDtypeStruct((1, rows), F32),
            jax.ShapeDtypeStruct((rows, 1), F32),
            jax.ShapeDtypeStruct(stat.shape, F32),
        ],
        compiler_params=pltpu.CompilerParams(vmem_limit_bytes=VMEM),
        name="totals",
    )(pairs, queries, keys, stat)


def merge_kernel(halves, factor_ref, *refs):
    out_ref = refs[-1]
    rows = out_ref.shape[0]
    wide = spread(factor_ref[...], rows)
    factor_all, factor_pos = column_of(wide, 0), column_of(wide, 1)
    step = pl.program_id(0)
    per = pl.num_programs(0) // halves
    for h in range(halves):

        @pl.when(step // per == h)
        def _():
            out_ref[...] = (
                factor_all * refs[2 * h][...] - factor_pos * refs[2 * h + 1][...]
            ).astype(BF16)


def merge(factors, parts):
    halves = len(parts)
    count, width = parts[0][0].shape
    step = 256
    per = count // step

    def place(h):
        return lambda i: (jnp.clip(i - h * per, 0, per - 1), 0)

    def kernel(*refs):
        merge_kernel(halves, *refs)

    return pl.pallas_call(
        kernel,
        grid=(halves * per,),
        in_specs=[pl.BlockSpec((step // 16, LANES), lambda i: (i, 0))]
        + [pl.BlockSpec((step, width), place(h)) for h in range(halves) for _ in range(2)],
        out_specs=pl.BlockSpec((step, width), lambda i: (i, 0)),
        out_shape=jax.ShapeDtypeStruct((halves * count, width), BF16),
        compiler_params=pltpu.CompilerParams(vmem_limit_bytes=VMEM),
        name="merge",
    )(factors, *[array for part in parts for array in part])


def gradient_kernel(pairs_ref, factor_ref, key_ref, back_ref, out_ref):
    step = pl.program_id(0)
    rows = key_ref.shape[0]
    chunk = back_ref.shape[0]
    block = iota((rows, 1), 0) >> 3
    place = iota((rows, chunk), 1) + step * chunk
    match = jnp.zeros((rows, chunk), F32)
    for k in range(pairs_ref.shape[1]):
        match = jnp.where(targets(pairs_ref, k, block) == (place >> 4), 1.0, match)
    side = (rows, rows)
    earlier = ((iota(side, 1) >> 3) < (iota(side, 0) >> 3)) & ((iota(side, 1) & 7) == 0)
    count = jnp.dot(earlier.astype(F32).astype(BF16), match.astype(BF16), preferred_element_type=F32)
    chosen = jnp.where(count == ((place >> 3) & 1).astype(F32), match, 0.0)
    chosen = jnp.where((place & 7) == (iota((rows, chunk), 0) & 7), chosen, 0.0)

    @pl.when(step == 0)
    def _():
        out_ref[...] = factor_ref[...] * key_ref[...].astype(F32)

    out_ref[...] += jnp.dot(chosen.astype(BF16), back_ref[...], preferred_element_type=F32)


def gradient(pairs, factor, keys, back):
    rows, width = keys.shape
    total = back.shape[0]
    chunk = 512
    return pl.pallas_call(
        gradient_kernel,
        grid=(total // chunk,),
        in_specs=[
            pl.BlockSpec(memory_space=pltpu.SMEM),
            pl.BlockSpec((rows, 1), lambda i: (0, 0)),
            pl.BlockSpec((rows, width), lambda i: (0, 0)),
            pl.BlockSpec((chunk, width), lambda i: (i, 0)),
        ],
        out_specs=pl.BlockSpec((rows, width), lambda i: (0, 0)),
        out_shape=jax.ShapeDtypeStruct((rows, width), F32),
        compiler_params=pltpu.CompilerParams(vmem_limit_bytes=VMEM),
        name="gradient",
    )(pairs, factor, keys, back)


def enqueue_kernel(slots, offset_ref, key_ref, memory_ref, out_ref):
    rows = memory_ref.shape[0]
    count = key_ref.shape[0]
    distance = iota((rows, 1), 0) + (pl.program_id(0) * rows - offset_ref[0] + slots)
    distance = jnp.where(distance >= slots, distance - slots, distance)
    lead = lax.rem(pl.program_id(0) * rows - offset_ref[0] + slots, slots)
    out_ref[...] = memory_ref[...]

    @pl.when((lead < count) | (lead + rows > slots))
    def _():
        pick = (distance == iota((rows, count), 1)).astype(F32).astype(BF16)
        fresh = jnp.dot(pick, key_ref[...], preferred_element_type=F32)
        out_ref[...] = jnp.where(distance < count, fresh, memory_ref[...].astype(F32)).astype(BF16)


def enqueue(offset, keys, memory):
    slots, width = memory.shape
    count = keys.shape[0]
    step = 256

    def kernel(*refs):
        enqueue_kernel(slots, *refs)

    return pl.pallas_call(
        kernel,
        grid=(slots // step,),
        in_specs=[
            pl.BlockSpec(memory_space=pltpu.SMEM),
            pl.BlockSpec((count, width), lambda i: (0, 0)),
            pl.BlockSpec((step, width), lambda i: (i, 0)),
        ],
        out_specs=pl.BlockSpec((step, width), lambda i: (i, 0)),
        out_shape=jax.ShapeDtypeStruct((slots, width), BF16),
        compiler_params=pltpu.CompilerParams(vmem_limit_bytes=VMEM),
        name="enqueue",
    )(offset, keys, memory)


def exchange(rows, per):
    shards = lax.axis_size(AXES)
    grouped = rows.reshape(shards, per, rows.shape[1])
    moved = lax.all_to_all(grouped, AXES, split_axis=0, concat_axis=0, tiled=True)
    return moved.reshape(rows.shape)


def body(queries, keys, labels, memory, mem_labels, pairs, offset):
    shards = lax.axis_size(AXES)
    rows_dev, width = queries.shape
    slots = memory.shape[0]
    slot_label = mem_labels.reshape(1, slots)
    send_query, send_label = pack(pairs, labels, queries, shards)
    rows_label = exchange(send_label, 1)
    rows_query = exchange(send_query, 16)
    updated = enqueue(offset, keys, memory)
    weights, stat = score(rows_query, rows_label, memory, slot_label)
    half = shards * 8
    stat = exchange(stat, 1)
    parts = [sums(weights, rows_label, memory, slot_label, first, half) for first in (0, half)]
    loss, factor, factors = totals(pairs, queries, keys, stat)
    factors = exchange(factors, 1)
    back = exchange(merge(factors, parts), 16)
    grad = gradient(pairs, factor, keys, back)
    return loss.reshape(rows_dev), grad, updated


def solution(mesh):
    in_specs = (
        P(AXES, None),
        P(AXES, None),
        P(AXES),
        P(AXES, None),
        P(AXES),
        P(AXES, None),
        P(),
    )
    out_specs = (P(AXES), P(AXES, None), P(AXES, None))
    return jax.shard_map(body, mesh=mesh, in_specs=in_specs, out_specs=out_specs, check_vma=False)
```

```python
import jax
import jax.numpy as jnp
from jax import lax
from jax.experimental import pallas as pl
from jax.experimental.pallas import tpu as pltpu
from jax.sharding import PartitionSpec as P

CAP = 2
F32 = jnp.float32
BF16 = jnp.bfloat16
I32 = jnp.int32
AXES = ("mem", "grp")
LANES = 128
MIB = 1024 * 1024
OWNER_STEP = 512
OWNER_SUB = 256
OWNER_MIB = 26
MERGE_STEP = 512
MERGE_MIB = 16
EXACT = lax.Precision.HIGHEST


def iota(shape, axis):
    return lax.broadcasted_iota(I32, shape, axis)


def targets(pairs_ref, k, block_of):
    out = jnp.zeros(block_of.shape, I32)
    for b in range(pairs_ref.shape[1]):
        out = jnp.where(block_of == b, pairs_ref[k, b], out)
    return out


def spread(packed, rows):
    n = packed.shape[0]
    return jnp.broadcast_to(packed[:, None, :], (n, 16, LANES)).reshape(rows, LANES)


def column_of(wide, group):
    rows = wide.shape[0]
    pick = iota((rows, LANES), 1) == group * 16 + (iota((rows, LANES), 0) & 15)
    return jnp.sum(jnp.where(pick, wide, 0.0), axis=1, keepdims=True)


def pack_kernel(pairs_ref, label_ref, query_ref, send_ref, rows_ref, table_ref):
    step = pl.program_id(0)
    fanout, blocks = pairs_ref.shape
    rows_dev, width = query_ref.shape
    shards = table_ref.shape[0] // CAP

    @pl.when(step == 0)
    def _():
        rows_ref[0:rows_dev, 0:width] = query_ref[...].astype(F32)
        side = (rows_dev, rows_dev)
        label = jnp.where(iota(side, 0) == iota(side, 1), label_ref[...].astype(F32), 0.0)
        label = jnp.sum(label, axis=1, keepdims=True)
        rows_ref[0:rows_dev, width:] = jnp.broadcast_to(label, (rows_dev, LANES))
        rows_ref[rows_dev:, :] = jnp.zeros((8, width + LANES), F32)

        def clear(i, carry):
            table_ref[i] = blocks
            return carry

        lax.fori_loop(0, shards * CAP, clear, 0)

        def enter(b, carry):
            for k in range(fanout):
                at = pairs_ref[k, b] * CAP
                at = at + jnp.where(table_ref[at] == blocks, 0, 1)
                table_ref[at] = b
            return carry

        lax.fori_loop(0, blocks, enter, 0)

    for j in range(send_ref.shape[0] // 16):
        at = (step * (send_ref.shape[0] // 16) + j) * CAP
        pair = [rows_ref[pl.ds(pl.multiple_of(table_ref[at + s] * 8, 8), 8), :] for s in range(CAP)]
        send_ref[j * 16 : (j + 1) * 16, :] = jnp.concatenate(pair, axis=0).astype(BF16)


def pack(pairs, labels, queries, shards):
    rows_dev, width = queries.shape
    step = 512
    return pl.pallas_call(
        pack_kernel,
        grid=(shards * 16 // step,),
        in_specs=[
            pl.BlockSpec(memory_space=pltpu.SMEM),
            pl.BlockSpec((1, rows_dev), lambda i: (0, 0)),
            pl.BlockSpec((rows_dev, width), lambda i: (0, 0)),
        ],
        out_specs=pl.BlockSpec((step, width + LANES), lambda i: (i, 0)),
        out_shape=jax.ShapeDtypeStruct((shards * 16, width + LANES), BF16),
        scratch_shapes=[
            pltpu.VMEM((rows_dev + 8, width + LANES), F32),
            pltpu.SMEM((shards * CAP,), I32),
        ],
        compiler_params=pltpu.CompilerParams(vmem_limit_bytes=16 * MIB),
        name="pack",
    )(pairs, labels.reshape(1, rows_dev), queries)


def owner_kernel(query_ref, memory_ref, slot_label_ref, all_ref, pos_ref, stat_ref):
    width = memory_ref.shape[1]
    sub = OWNER_SUB
    for c in range(query_ref.shape[0] // sub):
        at = slice(c * sub, (c + 1) * sub)
        scores = lax.dot_general(
            query_ref[at, 0:width], memory_ref[...], (((1,), (1,)), ((), ())), preferred_element_type=F32
        )
        top = jnp.max(scores, axis=1, keepdims=True)
        weights = jnp.exp(scores - top)
        row_label = query_ref[at, width : width + LANES].astype(F32)[:, 0:1]
        same = row_label == slot_label_ref[...].astype(F32)
        positive = jnp.where(same, weights, 0.0)
        part_all = jnp.sum(weights, axis=1, keepdims=True)
        part_pos = jnp.sum(positive, axis=1, keepdims=True)
        lane = iota((sub, LANES), 1)
        place = iota((sub, LANES), 0) & 15
        wide = jnp.where(lane == place, top, 0.0)
        wide = jnp.where(lane == place + 16, part_all, wide)
        wide = jnp.where(lane == place + 32, part_pos, wide)
        stat_ref[c * sub // 16 : (c + 1) * sub // 16, :] = jnp.sum(
            wide.reshape(sub // 16, 16, LANES), axis=1
        )
        both = jnp.dot(
            jnp.concatenate([weights.astype(BF16), positive.astype(BF16)], axis=0),
            memory_ref[...],
            preferred_element_type=F32,
        )
        all_ref[at, :] = both[:sub]
        pos_ref[at, :] = both[sub:]


def owner(rows_query, memory, slot_label):
    total = rows_query.shape[0]
    slots, width = memory.shape
    step = OWNER_STEP
    return pl.pallas_call(
        owner_kernel,
        grid=(total // step,),
        in_specs=[
            pl.BlockSpec((step, width + LANES), lambda i: (i, 0)),
            pl.BlockSpec((slots, width), lambda i: (0, 0), pipeline_mode=pl.Buffered(1)),
            pl.BlockSpec((1, slots), lambda i: (0, 0)),
        ],
        out_specs=[
            pl.BlockSpec((step, width), lambda i: (i, 0)),
            pl.BlockSpec((step, width), lambda i: (i, 0)),
            pl.BlockSpec((step // 16, LANES), lambda i: (i, 0)),
        ],
        out_shape=[
            jax.ShapeDtypeStruct((total, width), F32),
            jax.ShapeDtypeStruct((total, width), F32),
            jax.ShapeDtypeStruct((total // 16, LANES), F32),
        ],
        compiler_params=pltpu.CompilerParams(vmem_limit_bytes=OWNER_MIB * MIB),
        cost_estimate=pl.CostEstimate(
            flops=6 * total * slots * width, bytes_accessed=24 * MIB, transcendentals=total * slots
        ),
        name="owner",
    )(rows_query, memory, slot_label)


def total_kernel(pairs_ref, query_ref, key_ref, stat_ref, loss_ref, factor_ref, back_ref):
    rows = query_ref.shape[0]
    fanout = pairs_ref.shape[0]
    own = jnp.sum(query_ref[...].astype(F32) * key_ref[...].astype(F32), axis=1, keepdims=True)
    stat = stat_ref[...]
    stat_slot = (iota(stat.shape, 1) >> 3) & 1

    down_block = iota((rows, 1), 0) >> 3
    down_match = [
        (targets(pairs_ref, k, down_block) == iota((rows, LANES), 1)).astype(F32) for k in range(fanout)
    ]
    side = (rows, rows)
    earlier_down = ((iota(side, 1) >> 3) < (iota(side, 0) >> 3)) & ((iota(side, 1) & 7) == 0)
    down_count = jnp.dot(
        earlier_down.astype(F32).astype(BF16),
        sum(down_match[1:], down_match[0]).astype(BF16),
        preferred_element_type=F32,
    )
    lane = iota((rows, LANES), 1)
    mine = (lane & 7) == (iota((rows, LANES), 0) & 7)
    maxima, alls, poss = [], [], []
    for k in range(fanout):
        wide = jnp.zeros((rows, LANES), F32)
        for s in range(CAP):
            mask = jnp.where(down_count == s, down_match[k], 0.0)
            wide = wide + jnp.dot(
                mask, jnp.where(stat_slot == s, stat, 0.0), precision=EXACT, preferred_element_type=F32
            )
        for group, into in enumerate((maxima, alls, poss)):
            pick = mine & ((lane >> 4) == group)
            into.append(jnp.sum(jnp.where(pick, wide, 0.0), axis=1, keepdims=True))
    top = own
    for value in maxima:
        top = jnp.maximum(top, value)
    own_weight = jnp.exp(own - top)
    scales = [jnp.exp(value - top) for value in maxima]
    total_all, total_pos = own_weight, own_weight
    for k in range(fanout):
        total_all = total_all + scales[k] * alls[k]
        total_pos = total_pos + scales[k] * poss[k]
    loss = jnp.log(total_all) - jnp.log(total_pos)
    loss_ref[...] = jnp.sum(jnp.where(iota(side, 0) == iota(side, 1), loss, 0.0), axis=0, keepdims=True)
    factor_ref[...] = own_weight * (1.0 / total_all - 1.0 / total_pos)

    across_block = iota((1, rows), 1) >> 3
    across_match = [
        (targets(pairs_ref, k, across_block) == iota((LANES, rows), 0)).astype(F32) for k in range(fanout)
    ]
    earlier_across = ((iota(side, 0) >> 3) < (iota(side, 1) >> 3)) & ((iota(side, 0) & 7) == 0)
    across_count = jnp.dot(
        sum(across_match[1:], across_match[0]).astype(BF16),
        earlier_across.astype(F32).astype(BF16),
        preferred_element_type=F32,
    )
    back = jnp.zeros((LANES, LANES), F32)
    for k in range(fanout):
        factor_all, factor_pos = scales[k] / total_all, scales[k] / total_pos
        for s in range(CAP):
            mask = jnp.where(across_count == s, across_match[k], 0.0)
            value = jnp.where((lane >> 3) == s, factor_all, 0.0)
            value = jnp.where((lane >> 3) == 2 + s, factor_pos, value)
            value = jnp.where(mine, value, 0.0)
            back = back + jnp.dot(mask, value, precision=EXACT, preferred_element_type=F32)
    back_ref[...] = back


def totals(pairs, queries, keys, stat):
    rows = queries.shape[0]
    return pl.pallas_call(
        total_kernel,
        in_specs=[pl.BlockSpec(memory_space=pltpu.SMEM)] + [pl.BlockSpec(memory_space=pltpu.VMEM)] * 3,
        out_specs=[pl.BlockSpec(memory_space=pltpu.VMEM)] * 3,
        out_shape=[
            jax.ShapeDtypeStruct((1, rows), F32),
            jax.ShapeDtypeStruct((rows, 1), F32),
            jax.ShapeDtypeStruct(stat.shape, F32),
        ],
        compiler_params=pltpu.CompilerParams(vmem_limit_bytes=16 * MIB),
        name="totals",
    )(pairs, queries, keys, stat)


def merge_kernel(factor_ref, all_ref, pos_ref, out_ref):
    wide = spread(factor_ref[...], out_ref.shape[0])
    factor_all, factor_pos = column_of(wide, 0), column_of(wide, 1)
    out_ref[...] = (factor_all * all_ref[...] - factor_pos * pos_ref[...]).astype(BF16)


def merge(factors, sum_all, sum_pos):
    total, width = sum_all.shape
    step = MERGE_STEP
    return pl.pallas_call(
        merge_kernel,
        grid=(total // step,),
        in_specs=[pl.BlockSpec((step // 16, LANES), lambda i: (i, 0))]
        + [pl.BlockSpec((step, width), lambda i: (i, 0))] * 2,
        out_specs=pl.BlockSpec((step, width), lambda i: (i, 0)),
        out_shape=pltpu.HBM((total, width), BF16),
        compiler_params=pltpu.CompilerParams(vmem_limit_bytes=MERGE_MIB * MIB),
        name="merge",
    )(factors, sum_all, sum_pos)


def picker_kernel(pairs_ref, out_ref):
    rows, total = out_ref.shape
    block = iota((rows, 1), 0) >> 3
    place = iota((rows, total), 1)
    match = jnp.zeros((rows, total), F32)
    for k in range(pairs_ref.shape[0]):
        match = jnp.where(targets(pairs_ref, k, block) == (place >> 4), 1.0, match)
    side = (rows, rows)
    earlier = ((iota(side, 1) >> 3) < (iota(side, 0) >> 3)) & ((iota(side, 1) & 7) == 0)
    count = jnp.dot(earlier.astype(F32).astype(BF16), match.astype(BF16), preferred_element_type=F32)
    chosen = jnp.where(count == ((place >> 3) & 1).astype(F32), match, 0.0)
    chosen = jnp.where((place & 7) == (iota((rows, total), 0) & 7), chosen, 0.0)
    out_ref[...] = chosen.astype(BF16)


def picker(pairs, rows, total):
    return pl.pallas_call(
        picker_kernel,
        in_specs=[pl.BlockSpec(memory_space=pltpu.SMEM)],
        out_specs=pl.BlockSpec(memory_space=pltpu.VMEM),
        out_shape=jax.ShapeDtypeStruct((rows, total), BF16),
        compiler_params=pltpu.CompilerParams(vmem_limit_bytes=16 * MIB),
        name="picker",
    )(pairs)


def enqueue_kernel(slots, offset_ref, key_ref, memory_ref, out_ref):
    rows = memory_ref.shape[0]
    count = key_ref.shape[0]
    distance = iota((rows, 1), 0) + (pl.program_id(0) * rows - offset_ref[0] + slots)
    distance = jnp.where(distance >= slots, distance - slots, distance)
    lead = lax.rem(pl.program_id(0) * rows - offset_ref[0] + slots, slots)
    out_ref[...] = memory_ref[...]

    @pl.when((lead < count) | (lead + rows > slots))
    def _():
        pick = (distance == iota((rows, count), 1)).astype(F32).astype(BF16)
        fresh = jnp.dot(pick, key_ref[...], preferred_element_type=F32)
        out_ref[...] = jnp.where(distance < count, fresh, memory_ref[...].astype(F32)).astype(BF16)


def enqueue(offset, keys, memory):
    slots, width = memory.shape
    count = keys.shape[0]
    step = 512

    def kernel(*refs):
        enqueue_kernel(slots, *refs)

    return pl.pallas_call(
        kernel,
        grid=(slots // step,),
        in_specs=[
            pl.BlockSpec(memory_space=pltpu.SMEM),
            pl.BlockSpec((count, width), lambda i: (0, 0)),
            pl.BlockSpec((step, width), lambda i: (i, 0)),
        ],
        out_specs=pl.BlockSpec((step, width), lambda i: (i, 0)),
        out_shape=jax.ShapeDtypeStruct((slots, width), BF16),
        compiler_params=pltpu.CompilerParams(vmem_limit_bytes=24 * MIB),
        name="enqueue",
    )(offset, keys, memory)


def exchange(rows, per):
    shards = lax.axis_size(AXES)
    grouped = rows.reshape(shards, per, rows.shape[1])
    moved = lax.all_to_all(grouped, AXES, split_axis=0, concat_axis=0, tiled=True)
    return moved.reshape(rows.shape)


def body(queries, keys, labels, memory, mem_labels, pairs, offset):
    shards = lax.axis_size(AXES)
    rows_dev, width = queries.shape
    slots = memory.shape[0]
    slot_label = mem_labels.reshape(1, slots)
    pairs = pairs.T
    rows_query = exchange(pack(pairs, labels, queries, shards), 16)
    sum_all, sum_pos, stat = owner(rows_query, memory, slot_label)
    loss, factor, factors = totals(pairs, queries, keys, exchange(stat, 1))
    back = merge(exchange(factors, 1), sum_all, sum_pos)
    back, held, pairs = lax.optimization_barrier((back, memory, pairs))
    back = exchange(back, 16)
    updated = enqueue(offset, keys, held)
    picked = picker(pairs, rows_dev, shards * 16)
    grad = jnp.dot(picked, back, preferred_element_type=F32) + factor * keys.astype(F32)
    return loss.reshape(rows_dev), grad, updated


def solution(mesh):
    in_specs = (
        P(AXES, None),
        P(AXES, None),
        P(AXES),
        P(AXES, None),
        P(AXES),
        P(AXES, None),
        P(),
    )
    out_specs = (P(AXES), P(AXES, None), P(AXES, None))
    return jax.shard_map(body, mesh=mesh, in_specs=in_specs, out_specs=out_specs, check_vma=False)
```

```python
import jax
import jax.numpy as jnp
from jax import lax
from jax.experimental import pallas as pl
from jax.experimental.pallas import tpu as pltpu
from jax.sharding import PartitionSpec as P

CAP = 2
F32 = jnp.float32
BF16 = jnp.bfloat16
I32 = jnp.int32
AXES = ("mem", "grp")
LANES = 128
MIB = 1024 * 1024
OWNER_STEP = 512
OWNER_SUB = 256
OWNER_MIB = 26
MERGE_STEP = 512
MERGE_MIB = 16
EXACT = lax.Precision.HIGHEST


def iota(shape, axis):
    return lax.broadcasted_iota(I32, shape, axis)


def targets(pairs_ref, k, block_of):
    out = jnp.zeros(block_of.shape, I32)
    for b in range(pairs_ref.shape[1]):
        out = jnp.where(block_of == b, pairs_ref[k, b], out)
    return out


def spread(packed, rows):
    n = packed.shape[0]
    return jnp.broadcast_to(packed[:, None, :], (n, 16, LANES)).reshape(rows, LANES)


def column_of(wide, group):
    rows = wide.shape[0]
    pick = iota((rows, LANES), 1) == group * 16 + (iota((rows, LANES), 0) & 15)
    return jnp.sum(jnp.where(pick, wide, 0.0), axis=1, keepdims=True)


def pack_kernel(pairs_ref, label_ref, query_ref, send_ref, rows_ref, table_ref):
    fanout, blocks = pairs_ref.shape
    rows_dev, width = query_ref.shape
    shards = send_ref.shape[0]
    rows_ref[0:rows_dev, 0:width] = query_ref[...].astype(F32)
    side = (rows_dev, rows_dev)
    label = jnp.where(iota(side, 0) == iota(side, 1), label_ref[...].astype(F32), 0.0)
    label = jnp.sum(label, axis=1, keepdims=True)
    rows_ref[0:rows_dev, width:] = jnp.broadcast_to(label, (rows_dev, LANES))
    rows_ref[rows_dev:, :] = jnp.zeros((8, width + LANES), F32)

    def clear(i, carry):
        for u in range(16):
            table_ref[i * 16 + u] = blocks
        return carry

    lax.fori_loop(0, shards * CAP // 16, clear, 0)

    def enter(b, carry):
        for k in range(fanout):
            at = pairs_ref[k, b] * CAP
            at = at + jnp.where(table_ref[at] == blocks, 0, 1)
            table_ref[at] = b
        return carry

    lax.fori_loop(0, blocks, enter, 0)

    def fill(i, carry):
        for u in range(4):
            t = i * 4 + u
            pair = [
                rows_ref[pl.ds(pl.multiple_of(table_ref[t * CAP + s] * 8, 8), 8), :] for s in range(CAP)
            ]
            both = jnp.concatenate(pair, axis=0)
            for c in range(width // LANES):
                send_ref[t, c * 16 : (c + 1) * 16, :] = both[:, c * LANES : (c + 1) * LANES].astype(BF16)
            first, second = pair[0][:, width:], pair[1][:, width:]
            label = jnp.where(iota((8, LANES), 1) < LANES // 2, first, second)
            send_ref[t, width // 8 :, :] = label.astype(BF16)
        return carry

    lax.fori_loop(0, shards // 4, fill, 0)


def in_hbm(array):
    return pltpu.with_memory_space_constraint(array, pltpu.HBM)


def pack(pairs, labels, queries, shards):
    rows_dev, width = queries.shape
    return pl.pallas_call(
        pack_kernel,
        in_specs=[
            pl.BlockSpec(memory_space=pltpu.SMEM),
            pl.BlockSpec(memory_space=pltpu.VMEM),
            pl.BlockSpec(memory_space=pltpu.VMEM),
        ],
        out_specs=pl.BlockSpec(memory_space=pltpu.VMEM),
        out_shape=pltpu.VMEM((shards, width // 8 + 8, LANES), BF16),
        scratch_shapes=[
            pltpu.VMEM((rows_dev + 8, width + LANES), F32),
            pltpu.SMEM((shards * CAP,), I32),
        ],
        compiler_params=pltpu.CompilerParams(vmem_limit_bytes=16 * MIB),
        name="pack",
    )(in_hbm(pairs), in_hbm(labels.reshape(1, rows_dev)), in_hbm(queries))


def owner_kernel(query_ref, memory_ref, slot_label_ref, all_ref, pos_ref, stat_ref):
    width = memory_ref.shape[1]
    sub = OWNER_SUB
    for c in range(OWNER_STEP // sub):
        at = slice(c * sub, (c + 1) * sub)
        places = slice(c * sub // 16, (c + 1) * sub // 16)
        query = jnp.concatenate(
            [
                query_ref[places, i * 16 : (i + 1) * 16, :].reshape(sub, LANES)
                for i in range(width // LANES)
            ],
            axis=1,
        )
        label = query_ref[places, width // 8 :, :].astype(F32)
        half = LANES // 2
        label = jnp.concatenate([label[:, :, 0:half], label[:, :, half:]], axis=1)
        row_label = label.reshape(sub, half)[:, 0:1]
        scores = lax.dot_general(
            query, memory_ref[...], (((1,), (1,)), ((), ())), preferred_element_type=F32
        )
        top = jnp.max(scores, axis=1, keepdims=True)
        weights = jnp.exp(scores - top)
        same = row_label == slot_label_ref[...].astype(F32)
        positive = jnp.where(same, weights, 0.0)
        part_all = jnp.sum(weights, axis=1, keepdims=True)
        part_pos = jnp.sum(positive, axis=1, keepdims=True)
        lane = iota((sub, LANES), 1)
        place = iota((sub, LANES), 0) & 15
        wide = jnp.where(lane == place, top, 0.0)
        wide = jnp.where(lane == place + 16, part_all, wide)
        wide = jnp.where(lane == place + 32, part_pos, wide)
        stat_ref[c * sub // 16 : (c + 1) * sub // 16, :] = jnp.sum(
            wide.reshape(sub // 16, 16, LANES), axis=1
        )
        both = jnp.dot(
            jnp.concatenate([weights.astype(BF16), positive.astype(BF16)], axis=0),
            memory_ref[...],
            preferred_element_type=F32,
        )
        all_ref[at, :] = both[:sub]
        pos_ref[at, :] = both[sub:]


def owner(rows_query, memory, slot_label):
    shards, pieces = rows_query.shape[:2]
    total = shards * 16
    slots, width = memory.shape
    step = OWNER_STEP
    return pl.pallas_call(
        owner_kernel,
        grid=(total // step,),
        in_specs=[
            pl.BlockSpec((step // 16, pieces, LANES), lambda i: (i, 0, 0)),
            pl.BlockSpec((slots, width), lambda i: (0, 0), pipeline_mode=pl.Buffered(1)),
            pl.BlockSpec((1, slots), lambda i: (0, 0)),
        ],
        out_specs=[
            pl.BlockSpec((step, width), lambda i: (i, 0)),
            pl.BlockSpec((step, width), lambda i: (i, 0)),
            pl.BlockSpec((step // 16, LANES), lambda i: (i, 0)),
        ],
        out_shape=[
            jax.ShapeDtypeStruct((total, width), F32),
            jax.ShapeDtypeStruct((total, width), F32),
            jax.ShapeDtypeStruct((total // 16, LANES), F32),
        ],
        compiler_params=pltpu.CompilerParams(vmem_limit_bytes=OWNER_MIB * MIB),
        cost_estimate=pl.CostEstimate(
            flops=6 * total * slots * width, bytes_accessed=24 * MIB, transcendentals=total * slots
        ),
        name="owner",
    )(rows_query, memory, slot_label)


def total_kernel(pairs_ref, query_ref, key_ref, stat_ref, loss_ref, factor_ref, back_ref):
    rows = query_ref.shape[0]
    fanout = pairs_ref.shape[0]
    own = jnp.sum(query_ref[...].astype(F32) * key_ref[...].astype(F32), axis=1, keepdims=True)
    stat = stat_ref[...]
    stat_slot = (iota(stat.shape, 1) >> 3) & 1

    down_block = iota((rows, 1), 0) >> 3
    down_match = [
        (targets(pairs_ref, k, down_block) == iota((rows, LANES), 1)).astype(F32) for k in range(fanout)
    ]
    side = (rows, rows)
    earlier_down = ((iota(side, 1) >> 3) < (iota(side, 0) >> 3)) & ((iota(side, 1) & 7) == 0)
    down_count = jnp.dot(
        earlier_down.astype(F32).astype(BF16),
        sum(down_match[1:], down_match[0]).astype(BF16),
        preferred_element_type=F32,
    )
    lane = iota((rows, LANES), 1)
    mine = (lane & 7) == (iota((rows, LANES), 0) & 7)
    maxima, alls, poss = [], [], []
    for k in range(fanout):
        wide = jnp.zeros((rows, LANES), F32)
        for s in range(CAP):
            mask = jnp.where(down_count == s, down_match[k], 0.0)
            wide = wide + jnp.dot(
                mask, jnp.where(stat_slot == s, stat, 0.0), precision=EXACT, preferred_element_type=F32
            )
        for group, into in enumerate((maxima, alls, poss)):
            pick = mine & ((lane >> 4) == group)
            into.append(jnp.sum(jnp.where(pick, wide, 0.0), axis=1, keepdims=True))
    top = own
    for value in maxima:
        top = jnp.maximum(top, value)
    own_weight = jnp.exp(own - top)
    scales = [jnp.exp(value - top) for value in maxima]
    total_all, total_pos = own_weight, own_weight
    for k in range(fanout):
        total_all = total_all + scales[k] * alls[k]
        total_pos = total_pos + scales[k] * poss[k]
    loss = jnp.log(total_all) - jnp.log(total_pos)
    loss_ref[...] = jnp.sum(jnp.where(iota(side, 0) == iota(side, 1), loss, 0.0), axis=0, keepdims=True)
    factor_ref[...] = own_weight * (1.0 / total_all - 1.0 / total_pos)

    across_block = iota((1, rows), 1) >> 3
    across_match = [
        (targets(pairs_ref, k, across_block) == iota((LANES, rows), 0)).astype(F32) for k in range(fanout)
    ]
    earlier_across = ((iota(side, 0) >> 3) < (iota(side, 1) >> 3)) & ((iota(side, 0) & 7) == 0)
    across_count = jnp.dot(
        sum(across_match[1:], across_match[0]).astype(BF16),
        earlier_across.astype(F32).astype(BF16),
        preferred_element_type=F32,
    )
    back = jnp.zeros((LANES, LANES), F32)
    for k in range(fanout):
        factor_all, factor_pos = scales[k] / total_all, scales[k] / total_pos
        for s in range(CAP):
            mask = jnp.where(across_count == s, across_match[k], 0.0)
            value = jnp.where((lane >> 3) == s, factor_all, 0.0)
            value = jnp.where((lane >> 3) == 2 + s, factor_pos, value)
            value = jnp.where(mine, value, 0.0)
            back = back + jnp.dot(mask, value, precision=EXACT, preferred_element_type=F32)
    back_ref[...] = back


def totals(pairs, queries, keys, stat):
    rows = queries.shape[0]
    return pl.pallas_call(
        total_kernel,
        in_specs=[pl.BlockSpec(memory_space=pltpu.SMEM)] + [pl.BlockSpec(memory_space=pltpu.VMEM)] * 3,
        out_specs=[pl.BlockSpec(memory_space=pltpu.VMEM)] * 3,
        out_shape=[
            jax.ShapeDtypeStruct((1, rows), F32),
            jax.ShapeDtypeStruct((rows, 1), F32),
            jax.ShapeDtypeStruct(stat.shape, F32),
        ],
        compiler_params=pltpu.CompilerParams(vmem_limit_bytes=16 * MIB),
        name="totals",
    )(pairs, queries, keys, stat)


def merge_kernel(factor_ref, all_ref, pos_ref, out_ref):
    wide = spread(factor_ref[...], out_ref.shape[0])
    factor_all, factor_pos = column_of(wide, 0), column_of(wide, 1)
    out_ref[...] = (factor_all * all_ref[...] - factor_pos * pos_ref[...]).astype(BF16)


def merge(factors, sum_all, sum_pos):
    total, width = sum_all.shape
    step = MERGE_STEP
    return pl.pallas_call(
        merge_kernel,
        grid=(total // step,),
        in_specs=[pl.BlockSpec((step // 16, LANES), lambda i: (i, 0))]
        + [pl.BlockSpec((step, width), lambda i: (i, 0))] * 2,
        out_specs=pl.BlockSpec((step, width), lambda i: (i, 0)),
        out_shape=pltpu.HBM((total, width), BF16),
        compiler_params=pltpu.CompilerParams(vmem_limit_bytes=MERGE_MIB * MIB),
        name="merge",
    )(factors, sum_all, sum_pos)


def picker_kernel(pairs_ref, out_ref):
    rows, total = out_ref.shape
    block = iota((rows, 1), 0) >> 3
    place = iota((rows, total), 1)
    match = jnp.zeros((rows, total), F32)
    for k in range(pairs_ref.shape[0]):
        match = jnp.where(targets(pairs_ref, k, block) == (place >> 4), 1.0, match)
    side = (rows, rows)
    earlier = ((iota(side, 1) >> 3) < (iota(side, 0) >> 3)) & ((iota(side, 1) & 7) == 0)
    count = jnp.dot(earlier.astype(F32).astype(BF16), match.astype(BF16), preferred_element_type=F32)
    chosen = jnp.where(count == ((place >> 3) & 1).astype(F32), match, 0.0)
    chosen = jnp.where((place & 7) == (iota((rows, total), 0) & 7), chosen, 0.0)
    out_ref[...] = chosen.astype(BF16)


def picker(pairs, rows, total):
    return pl.pallas_call(
        picker_kernel,
        in_specs=[pl.BlockSpec(memory_space=pltpu.SMEM)],
        out_specs=pl.BlockSpec(memory_space=pltpu.VMEM),
        out_shape=jax.ShapeDtypeStruct((rows, total), BF16),
        compiler_params=pltpu.CompilerParams(vmem_limit_bytes=16 * MIB),
        name="picker",
    )(pairs)


def enqueue_kernel(slots, offset_ref, key_ref, memory_ref, out_ref):
    rows = memory_ref.shape[0]
    count = key_ref.shape[0]
    distance = iota((rows, 1), 0) + (pl.program_id(0) * rows - offset_ref[0] + slots)
    distance = jnp.where(distance >= slots, distance - slots, distance)
    lead = lax.rem(pl.program_id(0) * rows - offset_ref[0] + slots, slots)
    out_ref[...] = memory_ref[...]

    @pl.when((lead < count) | (lead + rows > slots))
    def _():
        pick = (distance == iota((rows, count), 1)).astype(F32).astype(BF16)
        fresh = jnp.dot(pick, key_ref[...], preferred_element_type=F32)
        out_ref[...] = jnp.where(distance < count, fresh, memory_ref[...].astype(F32)).astype(BF16)


def enqueue(offset, keys, memory):
    slots, width = memory.shape
    count = keys.shape[0]
    step = 512

    def kernel(*refs):
        enqueue_kernel(slots, *refs)

    return pl.pallas_call(
        kernel,
        grid=(slots // step,),
        in_specs=[
            pl.BlockSpec(memory_space=pltpu.SMEM),
            pl.BlockSpec((count, width), lambda i: (0, 0)),
            pl.BlockSpec((step, width), lambda i: (i, 0)),
        ],
        out_specs=pl.BlockSpec((step, width), lambda i: (i, 0)),
        out_shape=jax.ShapeDtypeStruct((slots, width), BF16),
        compiler_params=pltpu.CompilerParams(vmem_limit_bytes=24 * MIB),
        name="enqueue",
    )(offset, keys, memory)


def deal(groups):
    return lax.all_to_all(groups, AXES, split_axis=0, concat_axis=0, tiled=True)


def exchange(rows, per):
    shards = lax.axis_size(AXES)
    return deal(rows.reshape(shards, per, rows.shape[1])).reshape(rows.shape)


def body(queries, keys, labels, memory, mem_labels, pairs, offset):
    shards = lax.axis_size(AXES)
    rows_dev, width = queries.shape
    slots = memory.shape[0]
    slot_label = mem_labels.reshape(1, slots)
    pairs = pairs.T
    rows_query = deal(pack(pairs, labels, queries, shards))
    sum_all, sum_pos, stat = owner(rows_query, memory, slot_label)
    loss, factor, factors = totals(pairs, queries, keys, exchange(stat, 1))
    back = merge(exchange(factors, 1), sum_all, sum_pos)
    back, held, pairs = lax.optimization_barrier((back, memory, pairs))
    back = exchange(back, 16)
    updated = enqueue(offset, keys, held)
    picked = picker(pairs, rows_dev, shards * 16)
    grad = jnp.dot(picked, back, preferred_element_type=F32) + factor * keys.astype(F32)
    return loss.reshape(rows_dev), grad, updated


def solution(mesh):
    in_specs = (
        P(AXES, None),
        P(AXES, None),
        P(AXES),
        P(AXES, None),
        P(AXES),
        P(AXES, None),
        P(),
    )
    out_specs = (P(AXES), P(AXES, None), P(AXES, None))
    return jax.shard_map(body, mesh=mesh, in_specs=in_specs, out_specs=out_specs, check_vma=False)
```

```python
import jax
import jax.numpy as jnp
from jax import lax
from jax.experimental import pallas as pl
from jax.experimental.pallas import tpu as pltpu
from jax.sharding import PartitionSpec as P

CAP = 2
F32 = jnp.float32
BF16 = jnp.bfloat16
I32 = jnp.int32
AXES = ("mem", "grp")
LANES = 128
MIB = 1024 * 1024
OWNER_STEP = 512
OWNER_SUB = 256
OWNER_MIB = 26
MERGE_STEP = 1024
GRADIENT_CUTS = 4
MERGE_MIB = 28
EXACT = lax.Precision.HIGHEST


def iota(shape, axis):
    return lax.broadcasted_iota(I32, shape, axis)


def targets(pairs_ref, k, block_of):
    out = jnp.zeros(block_of.shape, I32)
    for b in range(pairs_ref.shape[1]):
        out = jnp.where(block_of == b, pairs_ref[k, b], out)
    return out


def spread(packed, rows):
    n = packed.shape[0]
    return jnp.broadcast_to(packed[:, None, :], (n, 16, LANES)).reshape(rows, LANES)


def column_of(wide, group):
    rows = wide.shape[0]
    pick = iota((rows, LANES), 1) == group * 16 + (iota((rows, LANES), 0) & 15)
    return jnp.sum(jnp.where(pick, wide, 0.0), axis=1, keepdims=True)


def pack_kernel(pairs_ref, label_ref, query_ref, send_ref, rows_ref, table_ref):
    fanout, blocks = pairs_ref.shape
    rows_dev, width = query_ref.shape
    shards = send_ref.shape[0]
    rows_ref[0:rows_dev, 0:width] = query_ref[...].astype(F32)
    side = (rows_dev, rows_dev)
    label = jnp.where(iota(side, 0) == iota(side, 1), label_ref[...].astype(F32), 0.0)
    label = jnp.sum(label, axis=1, keepdims=True)
    rows_ref[0:rows_dev, width:] = jnp.broadcast_to(label, (rows_dev, LANES))
    rows_ref[rows_dev:, :] = jnp.zeros((8, width + LANES), F32)

    def clear(i, carry):
        for u in range(16):
            table_ref[i * 16 + u] = blocks
        return carry

    lax.fori_loop(0, shards * CAP // 16, clear, 0)

    def enter(b, carry):
        for k in range(fanout):
            at = pairs_ref[k, b] * CAP
            at = at + jnp.where(table_ref[at] == blocks, 0, 1)
            table_ref[at] = b
        return carry

    lax.fori_loop(0, blocks, enter, 0)

    def fill(i, carry):
        for u in range(4):
            t = i * 4 + u
            pair = [
                rows_ref[pl.ds(pl.multiple_of(table_ref[t * CAP + s] * 8, 8), 8), :] for s in range(CAP)
            ]
            both = jnp.concatenate(pair, axis=0)
            for c in range(width // LANES):
                send_ref[t, c * 16 : (c + 1) * 16, :] = both[:, c * LANES : (c + 1) * LANES].astype(BF16)
            first, second = pair[0][:, width:], pair[1][:, width:]
            label = jnp.where(iota((8, LANES), 1) < LANES // 2, first, second)
            send_ref[t, width // 8 :, :] = label.astype(BF16)
        return carry

    lax.fori_loop(0, shards // 4, fill, 0)


def in_hbm(array):
    return pltpu.with_memory_space_constraint(array, pltpu.HBM)


def pack(pairs, labels, queries, shards):
    rows_dev, width = queries.shape
    return pl.pallas_call(
        pack_kernel,
        in_specs=[
            pl.BlockSpec(memory_space=pltpu.SMEM),
            pl.BlockSpec(memory_space=pltpu.VMEM),
            pl.BlockSpec(memory_space=pltpu.VMEM),
        ],
        out_specs=pl.BlockSpec(memory_space=pltpu.VMEM),
        out_shape=pltpu.VMEM((shards, width // 8 + 8, LANES), BF16),
        scratch_shapes=[
            pltpu.VMEM((rows_dev + 8, width + LANES), F32),
            pltpu.SMEM((shards * CAP,), I32),
        ],
        compiler_params=pltpu.CompilerParams(vmem_limit_bytes=16 * MIB),
        name="pack",
    )(in_hbm(pairs), in_hbm(labels.reshape(1, rows_dev)), in_hbm(queries))


def owner_kernel(query_ref, memory_ref, slot_label_ref, all_ref, pos_ref, stat_ref):
    width = memory_ref.shape[1]
    sub = OWNER_SUB
    for c in range(OWNER_STEP // sub):
        at = slice(c * sub, (c + 1) * sub)
        places = slice(c * sub // 16, (c + 1) * sub // 16)
        query = jnp.concatenate(
            [
                query_ref[places, i * 16 : (i + 1) * 16, :].reshape(sub, LANES)
                for i in range(width // LANES)
            ],
            axis=1,
        )
        label = query_ref[places, width // 8 :, :].astype(F32)
        half = LANES // 2
        label = jnp.concatenate([label[:, :, 0:half], label[:, :, half:]], axis=1)
        row_label = label.reshape(sub, half)[:, 0:1]
        scores = lax.dot_general(
            query, memory_ref[...], (((1,), (1,)), ((), ())), preferred_element_type=F32
        )
        top = jnp.max(scores, axis=1, keepdims=True)
        weights = jnp.exp(scores - top)
        same = row_label == slot_label_ref[...].astype(F32)
        positive = jnp.where(same, weights, 0.0)
        part_all = jnp.sum(weights, axis=1, keepdims=True)
        part_pos = jnp.sum(positive, axis=1, keepdims=True)
        lane = iota((sub, LANES), 1)
        place = iota((sub, LANES), 0) & 15
        wide = jnp.where(lane == place, top, 0.0)
        wide = jnp.where(lane == place + 16, part_all, wide)
        wide = jnp.where(lane == place + 32, part_pos, wide)
        stat_ref[c * sub // 16 : (c + 1) * sub // 16, :] = jnp.sum(
            wide.reshape(sub // 16, 16, LANES), axis=1
        )
        both = jnp.dot(
            jnp.concatenate([weights.astype(BF16), positive.astype(BF16)], axis=0),
            memory_ref[...],
            preferred_element_type=F32,
        )
        all_ref[at, :] = both[:sub]
        pos_ref[at, :] = both[sub:]


def owner(rows_query, memory, slot_label):
    shards, pieces = rows_query.shape[:2]
    total = shards * 16
    slots, width = memory.shape
    step = OWNER_STEP
    return pl.pallas_call(
        owner_kernel,
        grid=(total // step,),
        in_specs=[
            pl.BlockSpec((step // 16, pieces, LANES), lambda i: (i, 0, 0)),
            pl.BlockSpec((slots, width), lambda i: (0, 0), pipeline_mode=pl.Buffered(1)),
            pl.BlockSpec((1, slots), lambda i: (0, 0)),
        ],
        out_specs=[
            pl.BlockSpec((step, width), lambda i: (i, 0)),
            pl.BlockSpec((step, width), lambda i: (i, 0)),
            pl.BlockSpec((step // 16, LANES), lambda i: (i, 0)),
        ],
        out_shape=[
            jax.ShapeDtypeStruct((total, width), F32),
            jax.ShapeDtypeStruct((total, width), F32),
            jax.ShapeDtypeStruct((total // 16, LANES), F32),
        ],
        compiler_params=pltpu.CompilerParams(vmem_limit_bytes=OWNER_MIB * MIB),
        cost_estimate=pl.CostEstimate(
            flops=6 * total * slots * width, bytes_accessed=24 * MIB, transcendentals=total * slots
        ),
        name="owner",
    )(rows_query, memory, slot_label)


def total_kernel(pairs_ref, query_ref, key_ref, stat_ref, loss_ref, factor_ref, back_ref):
    rows = query_ref.shape[0]
    fanout = pairs_ref.shape[0]
    own = jnp.sum(query_ref[...].astype(F32) * key_ref[...].astype(F32), axis=1, keepdims=True)
    stat = stat_ref[...]
    stat_slot = (iota(stat.shape, 1) >> 3) & 1

    down_block = iota((rows, 1), 0) >> 3
    down_match = [
        (targets(pairs_ref, k, down_block) == iota((rows, LANES), 1)).astype(F32) for k in range(fanout)
    ]
    side = (rows, rows)
    earlier_down = ((iota(side, 1) >> 3) < (iota(side, 0) >> 3)) & ((iota(side, 1) & 7) == 0)
    down_count = jnp.dot(
        earlier_down.astype(F32).astype(BF16),
        sum(down_match[1:], down_match[0]).astype(BF16),
        preferred_element_type=F32,
    )
    lane = iota((rows, LANES), 1)
    mine = (lane & 7) == (iota((rows, LANES), 0) & 7)
    masks = [[jnp.where(down_count == s, match, 0.0) for s in range(CAP)] for match in down_match]
    wide = jnp.dot(
        jnp.concatenate([jnp.concatenate(mask, axis=1) for mask in masks], axis=0),
        jnp.concatenate([jnp.where(stat_slot == s, stat, 0.0) for s in range(CAP)], axis=0),
        precision=EXACT,
        preferred_element_type=F32,
    )
    maxima, alls, poss = [], [], []
    for k in range(fanout):
        part = wide[k * rows : (k + 1) * rows]
        for group, into in enumerate((maxima, alls, poss)):
            pick = mine & ((lane >> 4) == group)
            into.append(jnp.sum(jnp.where(pick, part, 0.0), axis=1, keepdims=True))
    top = own
    for value in maxima:
        top = jnp.maximum(top, value)
    own_weight = jnp.exp(own - top)
    scales = [jnp.exp(value - top) for value in maxima]
    total_all, total_pos = own_weight, own_weight
    for k in range(fanout):
        total_all = total_all + scales[k] * alls[k]
        total_pos = total_pos + scales[k] * poss[k]
    loss = jnp.log(total_all) - jnp.log(total_pos)
    loss_ref[...] = jnp.sum(jnp.where(iota(side, 0) == iota(side, 1), loss, 0.0), axis=0, keepdims=True)
    factor_ref[...] = own_weight * (1.0 / total_all - 1.0 / total_pos)

    values = []
    for k in range(fanout):
        factor_all = scales[k] / total_all
        factor_pos = jnp.where(total_pos > 0.0, scales[k] / total_pos, 0.0)
        for s in range(CAP):
            value = jnp.where((lane >> 3) == s, factor_all, 0.0)
            value = jnp.where((lane >> 3) == 2 + s, factor_pos, value)
            values.append(jnp.where(mine, value, 0.0))
    back_ref[...] = lax.dot_general(
        jnp.concatenate([mask for pair in masks for mask in pair], axis=0),
        jnp.concatenate(values, axis=0),
        (((0,), (0,)), ((), ())),
        precision=EXACT,
        preferred_element_type=F32,
    )


def totals(pairs, queries, keys, stat):
    rows = queries.shape[0]
    return pl.pallas_call(
        total_kernel,
        in_specs=[pl.BlockSpec(memory_space=pltpu.SMEM)] + [pl.BlockSpec(memory_space=pltpu.VMEM)] * 3,
        out_specs=[pl.BlockSpec(memory_space=pltpu.VMEM)] * 3,
        out_shape=[
            jax.ShapeDtypeStruct((1, rows), F32),
            jax.ShapeDtypeStruct((rows, 1), F32),
            jax.ShapeDtypeStruct(stat.shape, F32),
        ],
        compiler_params=pltpu.CompilerParams(vmem_limit_bytes=16 * MIB),
        name="totals",
    )(pairs, queries, keys, stat)


def merge_kernel(factor_ref, all_ref, pos_ref, out_ref):
    wide = spread(factor_ref[...], out_ref.shape[0])
    factor_all, factor_pos = column_of(wide, 0), column_of(wide, 1)
    out_ref[...] = (factor_all * all_ref[...] - factor_pos * pos_ref[...]).astype(BF16)


def merge(factors, sum_all, sum_pos):
    total, width = sum_all.shape
    step = MERGE_STEP
    return pl.pallas_call(
        merge_kernel,
        grid=(total // step,),
        in_specs=[pl.BlockSpec((step // 16, LANES), lambda i: (i, 0))]
        + [pl.BlockSpec((step, width), lambda i: (i, 0))] * 2,
        out_specs=pl.BlockSpec((step, width), lambda i: (i, 0)),
        out_shape=pltpu.HBM((total, width), BF16),
        compiler_params=pltpu.CompilerParams(vmem_limit_bytes=MERGE_MIB * MIB),
        name="merge",
    )(factors, sum_all, sum_pos)


def picker_kernel(pairs_ref, out_ref):
    rows, total = out_ref.shape
    block = iota((rows, 1), 0) >> 3
    place = iota((rows, total), 1)
    match = jnp.zeros((rows, total), F32)
    for k in range(pairs_ref.shape[0]):
        match = jnp.where(targets(pairs_ref, k, block) == (place >> 4), 1.0, match)
    side = (rows, rows)
    earlier = ((iota(side, 1) >> 3) < (iota(side, 0) >> 3)) & ((iota(side, 1) & 7) == 0)
    count = jnp.dot(earlier.astype(F32).astype(BF16), match.astype(BF16), preferred_element_type=F32)
    chosen = jnp.where(count == ((place >> 3) & 1).astype(F32), match, 0.0)
    chosen = jnp.where((place & 7) == (iota((rows, total), 0) & 7), chosen, 0.0)
    out_ref[...] = chosen.astype(BF16)


def picker(pairs, rows, total):
    return pl.pallas_call(
        picker_kernel,
        in_specs=[pl.BlockSpec(memory_space=pltpu.SMEM)],
        out_specs=pl.BlockSpec(memory_space=pltpu.VMEM),
        out_shape=jax.ShapeDtypeStruct((rows, total), BF16),
        compiler_params=pltpu.CompilerParams(vmem_limit_bytes=16 * MIB),
        name="picker",
    )(pairs)


def gradient_kernel(picked_ref, back_hbm, factor_ref, key_ref, out_ref, back_ref, sems):
    cuts = sems.shape[0]
    rows = back_ref.shape[0] // cuts

    def fetch(j):
        at = pl.ds(j * rows, rows)
        return pltpu.make_async_copy(back_hbm.at[at], back_ref.at[at], sems.at[j])

    parts = [fetch(j) for j in range(cuts)]
    for part in parts:
        part.start()
    total = factor_ref[...] * key_ref[...].astype(F32)
    for j in range(cuts):
        parts[j].wait()
        at = slice(j * rows, (j + 1) * rows)
        total = total + jnp.dot(picked_ref[:, at], back_ref[at, :], preferred_element_type=F32)
    out_ref[...] = total


def gradient(picked, back, factor, keys):
    return pl.pallas_call(
        gradient_kernel,
        in_specs=[
            pl.BlockSpec(memory_space=pltpu.VMEM),
            pl.BlockSpec(memory_space=pl.ANY),
            pl.BlockSpec(memory_space=pltpu.VMEM),
            pl.BlockSpec(memory_space=pltpu.VMEM),
        ],
        out_specs=pl.BlockSpec(memory_space=pltpu.VMEM),
        out_shape=jax.ShapeDtypeStruct(keys.shape, F32),
        scratch_shapes=[pltpu.VMEM(back.shape, BF16), pltpu.SemaphoreType.DMA((GRADIENT_CUTS,))],
        compiler_params=pltpu.CompilerParams(vmem_limit_bytes=16 * MIB),
        name="gradient",
    )(picked, back, factor, keys)


def enqueue_kernel(slots, offset_ref, key_ref, memory_ref, out_ref):
    rows = memory_ref.shape[0]
    count = key_ref.shape[0]
    distance = iota((rows, 1), 0) + (pl.program_id(0) * rows - offset_ref[0] + slots)
    distance = jnp.where(distance >= slots, distance - slots, distance)
    lead = lax.rem(pl.program_id(0) * rows - offset_ref[0] + slots, slots)
    out_ref[...] = memory_ref[...]

    @pl.when((lead < count) | (lead + rows > slots))
    def _():
        pick = (distance == iota((rows, count), 1)).astype(F32).astype(BF16)
        fresh = jnp.dot(pick, key_ref[...], preferred_element_type=F32)
        out_ref[...] = jnp.where(distance < count, fresh, memory_ref[...].astype(F32)).astype(BF16)


def enqueue(offset, keys, memory):
    slots, width = memory.shape
    count = keys.shape[0]
    step = 512

    def kernel(*refs):
        enqueue_kernel(slots, *refs)

    return pl.pallas_call(
        kernel,
        grid=(slots // step,),
        in_specs=[
            pl.BlockSpec(memory_space=pltpu.SMEM),
            pl.BlockSpec((count, width), lambda i: (0, 0)),
            pl.BlockSpec((step, width), lambda i: (i, 0)),
        ],
        out_specs=pl.BlockSpec((step, width), lambda i: (i, 0)),
        out_shape=jax.ShapeDtypeStruct((slots, width), BF16),
        compiler_params=pltpu.CompilerParams(vmem_limit_bytes=24 * MIB),
        name="enqueue",
    )(offset, keys, memory)


def deal(groups):
    return lax.all_to_all(groups, AXES, split_axis=0, concat_axis=0, tiled=True)


def exchange(rows, per):
    shards = lax.axis_size(AXES)
    return deal(rows.reshape(shards, per, rows.shape[1])).reshape(rows.shape)


def body(queries, keys, labels, memory, mem_labels, pairs, offset):
    shards = lax.axis_size(AXES)
    rows_dev, width = queries.shape
    slots = memory.shape[0]
    slot_label = mem_labels.reshape(1, slots)
    pairs = pairs.T
    rows_query = deal(pack(pairs, labels, queries, shards))
    sum_all, sum_pos, stat = owner(rows_query, memory, slot_label)
    loss, factor, factors = totals(pairs, queries, keys, exchange(stat, 1))
    back = merge(exchange(factors, 1), sum_all, sum_pos)
    back, held, pairs = lax.optimization_barrier((back, memory, pairs))
    back = exchange(back, 16)
    updated = enqueue(offset, keys, held)
    picked = picker(pairs, rows_dev, shards * 16)
    grad = gradient(picked, back, factor, keys)
    return loss.reshape(rows_dev), grad, updated


def solution(mesh):
    in_specs = (
        P(AXES, None),
        P(AXES, None),
        P(AXES),
        P(AXES, None),
        P(AXES),
        P(AXES, None),
        P(),
    )
    out_specs = (P(AXES), P(AXES, None), P(AXES, None))
    return jax.shard_map(body, mesh=mesh, in_specs=in_specs, out_specs=out_specs, check_vma=False)
```

```python
import jax
import jax.numpy as jnp
from jax import lax
from jax.experimental import pallas as pl
from jax.experimental.pallas import tpu as pltpu
from jax.sharding import PartitionSpec as P

CAP = 2
F32 = jnp.float32
BF16 = jnp.bfloat16
I32 = jnp.int32
AXES = ("mem", "grp")
LANES = 128
MIB = 1024 * 1024
OWNER_STEP = 2048
OWNER_SUB = 256
OWNER_MIB = 26
MERGE_STEP = 1024
GRADIENT_CUTS = 4
MERGE_MIB = 28
EXACT = lax.Precision.HIGHEST


def iota(shape, axis):
    return lax.broadcasted_iota(I32, shape, axis)


def targets(pairs_ref, k, block_of):
    out = jnp.zeros(block_of.shape, I32)
    for b in range(pairs_ref.shape[1]):
        out = jnp.where(block_of == b, pairs_ref[k, b], out)
    return out


def spread(packed, rows):
    n = packed.shape[0]
    return jnp.broadcast_to(packed[:, None, :], (n, 16, LANES)).reshape(rows, LANES)


def column_of(wide, group):
    rows = wide.shape[0]
    pick = iota((rows, LANES), 1) == group * 16 + (iota((rows, LANES), 0) & 15)
    return jnp.sum(jnp.where(pick, wide, 0.0), axis=1, keepdims=True)


def pack_kernel(pairs_ref, label_ref, query_ref, send_ref, rows_ref, table_ref):
    fanout, blocks = pairs_ref.shape
    rows_dev, width = query_ref.shape
    shards = send_ref.shape[0]
    rows_ref[0:rows_dev, 0:width] = query_ref[...].astype(F32)
    side = (rows_dev, rows_dev)
    label = jnp.where(iota(side, 0) == iota(side, 1), label_ref[...].astype(F32), 0.0)
    label = jnp.sum(label, axis=1, keepdims=True)
    rows_ref[0:rows_dev, width:] = jnp.broadcast_to(label, (rows_dev, LANES))
    rows_ref[rows_dev:, :] = jnp.zeros((8, width + LANES), F32)

    def clear(i, carry):
        for u in range(16):
            table_ref[i * 16 + u] = blocks
        return carry

    lax.fori_loop(0, shards * CAP // 16, clear, 0)

    def enter(b, carry):
        for k in range(fanout):
            at = pairs_ref[k, b] * CAP
            at = at + jnp.where(table_ref[at] == blocks, 0, 1)
            table_ref[at] = b
        return carry

    lax.fori_loop(0, blocks, enter, 0)

    def fill(i, carry):
        for u in range(4):
            t = i * 4 + u
            pair = [
                rows_ref[pl.ds(pl.multiple_of(table_ref[t * CAP + s] * 8, 8), 8), :] for s in range(CAP)
            ]
            both = jnp.concatenate(pair, axis=0)
            for c in range(width // LANES):
                send_ref[t, c * 16 : (c + 1) * 16, :] = both[:, c * LANES : (c + 1) * LANES].astype(BF16)
            first, second = pair[0][:, width:], pair[1][:, width:]
            label = jnp.where(iota((8, LANES), 1) < LANES // 2, first, second)
            send_ref[t, width // 8 :, :] = label.astype(BF16)
        return carry

    lax.fori_loop(0, shards // 4, fill, 0)


def in_hbm(array):
    return pltpu.with_memory_space_constraint(array, pltpu.HBM)


def pack(pairs, labels, queries, shards):
    rows_dev, width = queries.shape
    return pl.pallas_call(
        pack_kernel,
        in_specs=[
            pl.BlockSpec(memory_space=pltpu.SMEM),
            pl.BlockSpec(memory_space=pltpu.VMEM),
            pl.BlockSpec(memory_space=pltpu.VMEM),
        ],
        out_specs=pl.BlockSpec(memory_space=pltpu.VMEM),
        out_shape=pltpu.VMEM((shards, width // 8 + 8, LANES), BF16),
        scratch_shapes=[
            pltpu.VMEM((rows_dev + 8, width + LANES), F32),
            pltpu.SMEM((shards * CAP,), I32),
        ],
        compiler_params=pltpu.CompilerParams(vmem_limit_bytes=16 * MIB),
        name="pack",
    )(in_hbm(pairs), in_hbm(labels.reshape(1, rows_dev)), in_hbm(queries))


def owner_kernel(query_ref, memory_ref, slot_label_ref, all_ref, pos_ref, stat_ref):
    width = memory_ref.shape[1]
    sub = OWNER_SUB
    lead = pl.program_id(0) * OWNER_STEP
    for c in range(OWNER_STEP // sub):
        at = pl.ds(pl.multiple_of(lead + c * sub, sub), sub)
        places = slice(c * sub // 16, (c + 1) * sub // 16)
        query = jnp.concatenate(
            [
                query_ref[places, i * 16 : (i + 1) * 16, :].reshape(sub, LANES)
                for i in range(width // LANES)
            ],
            axis=1,
        )
        label = query_ref[places, width // 8 :, :].astype(F32)
        half = LANES // 2
        label = jnp.concatenate([label[:, :, 0:half], label[:, :, half:]], axis=1)
        row_label = label.reshape(sub, half)[:, 0:1]
        scores = lax.dot_general(
            query, memory_ref[...], (((1,), (1,)), ((), ())), preferred_element_type=F32
        )
        top = jnp.max(scores, axis=1, keepdims=True)
        weights = jnp.exp(scores - top)
        same = row_label == slot_label_ref[...].astype(F32)
        positive = jnp.where(same, weights, 0.0)
        part_all = jnp.sum(weights, axis=1, keepdims=True)
        part_pos = jnp.sum(positive, axis=1, keepdims=True)
        lane = iota((sub, LANES), 1)
        place = iota((sub, LANES), 0) & 15
        wide = jnp.where(lane == place, top, 0.0)
        wide = jnp.where(lane == place + 16, part_all, wide)
        wide = jnp.where(lane == place + 32, part_pos, wide)
        stat_ref[c * sub // 16 : (c + 1) * sub // 16, :] = jnp.sum(
            wide.reshape(sub // 16, 16, LANES), axis=1
        )
        both = jnp.dot(
            jnp.concatenate([weights.astype(BF16), positive.astype(BF16)], axis=0),
            memory_ref[...],
            preferred_element_type=F32,
        )
        all_ref[at, :] = both[:sub]
        pos_ref[at, :] = both[sub:]


def owner(rows_query, memory, slot_label):
    shards, pieces = rows_query.shape[:2]
    total = shards * 16
    slots, width = memory.shape
    step = OWNER_STEP
    return pl.pallas_call(
        owner_kernel,
        grid=(total // step,),
        in_specs=[
            pl.BlockSpec((step // 16, pieces, LANES), lambda i: (i, 0, 0)),
            pl.BlockSpec((slots, width), lambda i: (0, 0), pipeline_mode=pl.Buffered(1)),
            pl.BlockSpec((1, slots), lambda i: (0, 0)),
        ],
        out_specs=[
            pl.BlockSpec(memory_space=pltpu.VMEM),
            pl.BlockSpec(memory_space=pltpu.VMEM),
            pl.BlockSpec((step // 16, LANES), lambda i: (i, 0)),
        ],
        out_shape=[
            pltpu.VMEM((total, width), F32),
            pltpu.VMEM((total, width), F32),
            jax.ShapeDtypeStruct((total // 16, LANES), F32),
        ],
        compiler_params=pltpu.CompilerParams(vmem_limit_bytes=OWNER_MIB * MIB),
        cost_estimate=pl.CostEstimate(
            flops=6 * total * slots * width, bytes_accessed=24 * MIB, transcendentals=total * slots
        ),
        name="owner",
    )(rows_query, memory, slot_label)


def total_kernel(pairs_ref, query_ref, key_ref, stat_ref, loss_ref, factor_ref, back_ref):
    rows = query_ref.shape[0]
    fanout = pairs_ref.shape[0]
    own = jnp.sum(query_ref[...].astype(F32) * key_ref[...].astype(F32), axis=1, keepdims=True)
    stat = stat_ref[...]
    stat_slot = (iota(stat.shape, 1) >> 3) & 1

    down_block = iota((rows, 1), 0) >> 3
    down_match = [
        (targets(pairs_ref, k, down_block) == iota((rows, LANES), 1)).astype(F32) for k in range(fanout)
    ]
    side = (rows, rows)
    earlier_down = ((iota(side, 1) >> 3) < (iota(side, 0) >> 3)) & ((iota(side, 1) & 7) == 0)
    down_count = jnp.dot(
        earlier_down.astype(F32).astype(BF16),
        sum(down_match[1:], down_match[0]).astype(BF16),
        preferred_element_type=F32,
    )
    lane = iota((rows, LANES), 1)
    mine = (lane & 7) == (iota((rows, LANES), 0) & 7)
    masks = [[jnp.where(down_count == s, match, 0.0) for s in range(CAP)] for match in down_match]
    wide = jnp.dot(
        jnp.concatenate([jnp.concatenate(mask, axis=1) for mask in masks], axis=0),
        jnp.concatenate([jnp.where(stat_slot == s, stat, 0.0) for s in range(CAP)], axis=0),
        precision=EXACT,
        preferred_element_type=F32,
    )
    maxima, alls, poss = [], [], []
    for k in range(fanout):
        part = wide[k * rows : (k + 1) * rows]
        for group, into in enumerate((maxima, alls, poss)):
            pick = mine & ((lane >> 4) == group)
            into.append(jnp.sum(jnp.where(pick, part, 0.0), axis=1, keepdims=True))
    top = own
    for value in maxima:
        top = jnp.maximum(top, value)
    own_weight = jnp.exp(own - top)
    scales = [jnp.exp(value - top) for value in maxima]
    total_all, total_pos = own_weight, own_weight
    for k in range(fanout):
        total_all = total_all + scales[k] * alls[k]
        total_pos = total_pos + scales[k] * poss[k]
    loss = jnp.log(total_all) - jnp.log(total_pos)
    loss_ref[...] = jnp.sum(jnp.where(iota(side, 0) == iota(side, 1), loss, 0.0), axis=0, keepdims=True)
    factor_ref[...] = own_weight * (1.0 / total_all - 1.0 / total_pos)

    values = []
    for k in range(fanout):
        factor_all = scales[k] / total_all
        factor_pos = jnp.where(total_pos > 0.0, scales[k] / total_pos, 0.0)
        for s in range(CAP):
            value = jnp.where((lane >> 3) == s, factor_all, 0.0)
            value = jnp.where((lane >> 3) == 2 + s, factor_pos, value)
            values.append(jnp.where(mine, value, 0.0))
    back_ref[...] = lax.dot_general(
        jnp.concatenate([mask for pair in masks for mask in pair], axis=0),
        jnp.concatenate(values, axis=0),
        (((0,), (0,)), ((), ())),
        precision=EXACT,
        preferred_element_type=F32,
    )


def totals(pairs, queries, keys, stat):
    rows = queries.shape[0]
    return pl.pallas_call(
        total_kernel,
        in_specs=[pl.BlockSpec(memory_space=pltpu.SMEM)] + [pl.BlockSpec(memory_space=pltpu.VMEM)] * 3,
        out_specs=[pl.BlockSpec(memory_space=pltpu.VMEM)] * 3,
        out_shape=[
            jax.ShapeDtypeStruct((1, rows), F32),
            jax.ShapeDtypeStruct((rows, 1), F32),
            jax.ShapeDtypeStruct(stat.shape, F32),
        ],
        compiler_params=pltpu.CompilerParams(vmem_limit_bytes=16 * MIB),
        name="totals",
    )(pairs, queries, keys, stat)


def merge_kernel(factor_ref, all_ref, pos_ref, out_ref):
    wide = spread(factor_ref[...], out_ref.shape[0])
    factor_all, factor_pos = column_of(wide, 0), column_of(wide, 1)
    out_ref[...] = (factor_all * all_ref[...] - factor_pos * pos_ref[...]).astype(BF16)


def merge(factors, sum_all, sum_pos):
    total, width = sum_all.shape
    step = MERGE_STEP
    return pl.pallas_call(
        merge_kernel,
        grid=(total // step,),
        in_specs=[pl.BlockSpec((step // 16, LANES), lambda i: (i, 0))]
        + [pl.BlockSpec((step, width), lambda i: (i, 0))] * 2,
        out_specs=pl.BlockSpec((step, width), lambda i: (i, 0)),
        out_shape=pltpu.HBM((total, width), BF16),
        compiler_params=pltpu.CompilerParams(vmem_limit_bytes=MERGE_MIB * MIB),
        name="merge",
    )(factors, sum_all, sum_pos)


def picker_kernel(pairs_ref, out_ref):
    rows, total = out_ref.shape
    block = iota((rows, 1), 0) >> 3
    place = iota((rows, total), 1)
    match = jnp.zeros((rows, total), F32)
    for k in range(pairs_ref.shape[0]):
        match = jnp.where(targets(pairs_ref, k, block) == (place >> 4), 1.0, match)
    side = (rows, rows)
    earlier = ((iota(side, 1) >> 3) < (iota(side, 0) >> 3)) & ((iota(side, 1) & 7) == 0)
    count = jnp.dot(earlier.astype(F32).astype(BF16), match.astype(BF16), preferred_element_type=F32)
    chosen = jnp.where(count == ((place >> 3) & 1).astype(F32), match, 0.0)
    chosen = jnp.where((place & 7) == (iota((rows, total), 0) & 7), chosen, 0.0)
    out_ref[...] = chosen.astype(BF16)


def picker(pairs, rows, total):
    return pl.pallas_call(
        picker_kernel,
        in_specs=[pl.BlockSpec(memory_space=pltpu.SMEM)],
        out_specs=pl.BlockSpec(memory_space=pltpu.VMEM),
        out_shape=jax.ShapeDtypeStruct((rows, total), BF16),
        compiler_params=pltpu.CompilerParams(vmem_limit_bytes=16 * MIB),
        name="picker",
    )(pairs)


def gradient_kernel(picked_ref, back_hbm, factor_ref, key_ref, out_ref, back_ref, sems):
    cuts = sems.shape[0]
    rows = back_ref.shape[0] // cuts

    def fetch(j):
        at = pl.ds(j * rows, rows)
        return pltpu.make_async_copy(back_hbm.at[at], back_ref.at[at], sems.at[j])

    parts = [fetch(j) for j in range(cuts)]
    for part in parts:
        part.start()
    total = factor_ref[...] * key_ref[...].astype(F32)
    for j in range(cuts):
        parts[j].wait()
        at = slice(j * rows, (j + 1) * rows)
        total = total + jnp.dot(picked_ref[:, at], back_ref[at, :], preferred_element_type=F32)
    out_ref[...] = total


def gradient(picked, back, factor, keys):
    return pl.pallas_call(
        gradient_kernel,
        in_specs=[
            pl.BlockSpec(memory_space=pltpu.VMEM),
            pl.BlockSpec(memory_space=pl.ANY),
            pl.BlockSpec(memory_space=pltpu.VMEM),
            pl.BlockSpec(memory_space=pltpu.VMEM),
        ],
        out_specs=pl.BlockSpec(memory_space=pltpu.VMEM),
        out_shape=jax.ShapeDtypeStruct(keys.shape, F32),
        scratch_shapes=[pltpu.VMEM(back.shape, BF16), pltpu.SemaphoreType.DMA((GRADIENT_CUTS,))],
        compiler_params=pltpu.CompilerParams(vmem_limit_bytes=16 * MIB),
        name="gradient",
    )(picked, back, factor, keys)


def enqueue_kernel(slots, offset_ref, key_ref, memory_ref, out_ref):
    rows = memory_ref.shape[0]
    count = key_ref.shape[0]
    distance = iota((rows, 1), 0) + (pl.program_id(0) * rows - offset_ref[0] + slots)
    distance = jnp.where(distance >= slots, distance - slots, distance)
    lead = lax.rem(pl.program_id(0) * rows - offset_ref[0] + slots, slots)
    out_ref[...] = memory_ref[...]

    @pl.when((lead < count) | (lead + rows > slots))
    def _():
        pick = (distance == iota((rows, count), 1)).astype(F32).astype(BF16)
        fresh = jnp.dot(pick, key_ref[...], preferred_element_type=F32)
        out_ref[...] = jnp.where(distance < count, fresh, memory_ref[...].astype(F32)).astype(BF16)


def enqueue(offset, keys, memory):
    slots, width = memory.shape
    count = keys.shape[0]
    step = 512

    def kernel(*refs):
        enqueue_kernel(slots, *refs)

    return pl.pallas_call(
        kernel,
        grid=(slots // step,),
        in_specs=[
            pl.BlockSpec(memory_space=pltpu.SMEM),
            pl.BlockSpec((count, width), lambda i: (0, 0)),
            pl.BlockSpec((step, width), lambda i: (i, 0)),
        ],
        out_specs=pl.BlockSpec((step, width), lambda i: (i, 0)),
        out_shape=jax.ShapeDtypeStruct((slots, width), BF16),
        compiler_params=pltpu.CompilerParams(vmem_limit_bytes=24 * MIB),
        name="enqueue",
    )(offset, keys, memory)


def deal(groups):
    return lax.all_to_all(groups, AXES, split_axis=0, concat_axis=0, tiled=True)


def exchange(rows, per):
    shards = lax.axis_size(AXES)
    return deal(rows.reshape(shards, per, rows.shape[1])).reshape(rows.shape)


def body(queries, keys, labels, memory, mem_labels, pairs, offset):
    shards = lax.axis_size(AXES)
    rows_dev, width = queries.shape
    slots = memory.shape[0]
    slot_label = mem_labels.reshape(1, slots)
    pairs = pairs.T
    rows_query = deal(pack(pairs, labels, queries, shards))
    sum_all, sum_pos, stat = owner(rows_query, memory, slot_label)
    loss, factor, factors = totals(pairs, queries, keys, exchange(stat, 1))
    back = merge(exchange(factors, 1), sum_all, sum_pos)
    back, held, pairs = lax.optimization_barrier((back, memory, pairs))
    back = exchange(back, 16)
    updated = enqueue(offset, keys, held)
    picked = picker(pairs, rows_dev, shards * 16)
    grad = gradient(picked, back, factor, keys)
    return loss.reshape(rows_dev), grad, updated


def solution(mesh):
    in_specs = (
        P(AXES, None),
        P(AXES, None),
        P(AXES),
        P(AXES, None),
        P(AXES),
        P(AXES, None),
        P(),
    )
    out_specs = (P(AXES), P(AXES, None), P(AXES, None))
    return jax.shard_map(body, mesh=mesh, in_specs=in_specs, out_specs=out_specs, check_vma=False)
```
